512 devices in a mesh: ulysses: 8 (over y_lo, core), blk: 64 (over z, y_hi, x).
Axes of the slice: x: 4, y: 8 (y_hi: 2, y_lo: 4; y = y_hi * 4 + y_lo), z: 8, core: 2. Of those that a mesh axis runs over, the one named last changes fastest.
Arguments:
- queries: bfloat16 [65536, 4096], P(('ulysses', 'blk')), may hold values from -6 to 6
- keys: bfloat16 [65536, 512], P(('ulysses', 'blk')), may hold values from -6 to 6
- values: bfloat16 [65536, 512], P(('ulysses', 'blk')), may hold values from -6 to 6
- grad_out: bfloat16 [65536, 4096], P(('ulysses', 'blk')), may hold values from -6 to 6
- attn_out: bfloat16 [8, 8192, 4096], P(None, 'blk', 'ulysses'), may hold values from -2 to 2
- log_norm: float32 [8, 32, 8192], P(None, 'ulysses', 'blk'), may hold values from 3 to 5
- doc_start: int32 [8, 8192], P(None, 'blk'), may hold values from 0 to 65535, as said below
Outputs:
- grad_queries: bfloat16 [65536, 4096], P(('ulysses', 'blk'))
- grad_keys: bfloat16 [65536, 512], P(('ulysses', 'blk'))
- grad_values: bfloat16 [65536, 512], P(('ulysses', 'blk'))
The draws below stay inside these ranges and needn't reach their ends.
Inputs may be any that keep to these rules, and one draw needn't show every extreme that they name: doc_start[t] is the first position of the document that holds position t: it is t itself or equals doc_start of position t - 1, it is 0 at position 0, and the last position begins a document of its own.
All inputs are finite; a program needn't handle non-finite values.
Results may differ from the reference program's by a relative error of at most 0.012.
Values may be sent and summed in bfloat16 or wider, within the bound.
No kernel may reach another device: no remote copies, remote signals or barrier semaphores. Data moves between devices by JAX's collectives and lax.ppermute only.
A program may use at most 64 MiB of HBM per device.

```python
import jax
import jax.numpy as jnp
from jax import lax

HQ = 32
KVH = 4
DH = 128
TOK_DEV = 128
TOKENS = 65536
N_ULYSSES = 8
N_BLK = 64


def draw_doc_start(key, part):
    key = jax.random.fold_in(key, 11)
    total = N_ULYSSES * N_BLK * TOK_DEV
    marks = jax.random.randint(key, (total,), 0, 2 * TOK_DEV) == 0
    where_at = jnp.arange(total, dtype=jnp.int32)
    marks = marks | (where_at == 0) | (where_at == total - 1)
    starts = jnp.where(marks, where_at, 0)
    return lax.cummax(starts).reshape(N_ULYSSES, N_BLK * TOK_DEV)


def levels(rng, extent, cuts, smallest, high):
    def one(position, shards_of):
        heights = jax.random.uniform(jax.random.fold_in(jax.random.fold_in(rng, 6), position), (shards_of,), jnp.float32, smallest / len(cuts), high / len(cuts))
        return jnp.repeat(jnp.exp(heights), extent[position] // shards_of).reshape((-1,) + (1,) * (len(extent) - position - 1))

    factor_of = one(*cuts[0])
    for cut in cuts[1:]:
        factor_of = factor_of * one(*cut)
    return factor_of


def gaussian(stream_key, dims, deviation, limit, cuts=(), kind=jnp.bfloat16):
    array = deviation * jax.random.normal(stream_key, dims, jnp.float32)
    if cuts:
        array = array * levels(stream_key, dims, cuts, -0.22, 0.18)
    return jnp.clip(array, -limit, limit).astype(kind)


def setup_inputs(seed: int = 0) -> dict:
    key_of = jax.random.split(jax.random.key(seed), 8)
    return {
        "queries": gaussian(key_of[0], (TOKENS, HQ * DH), 1.0, 6.0, ((0, 512),)),
        "keys": gaussian(key_of[1], (TOKENS, KVH * DH), 1.0, 6.0, ((0, 512),)),
        "values": gaussian(key_of[2], (TOKENS, KVH * DH), 1.0, 6.0, ((0, 512),)),
        "grad_out": gaussian(key_of[3], (TOKENS, HQ * DH), 1.0, 6.0, ((0, 512),)),
        "attn_out": gaussian(key_of[4], (N_ULYSSES, N_BLK * TOK_DEV, HQ * DH), 0.3, 2.0, ((1, 64), (2, 8))),
        "log_norm": jnp.clip(3.0 + 2.0 * jax.random.uniform(key_of[5], (N_ULYSSES, HQ, N_BLK * TOK_DEV), jnp.float32) ** levels(key_of[5], (N_ULYSSES, HQ, N_BLK * TOK_DEV), ((1, 8), (2, 64)), -0.2, 0.2), 3.0, 5.0),
        "doc_start": draw_doc_start(jax.random.fold_in(key_of[7], 71), 0),
    }


def reference(queries, keys, values, grad_out, attn_out, log_norm, doc_start):
    length = queries.shape[0]
    block_rows = TOK_DEV
    window = 3 * TOK_DEV // 2
    score_scale = DH ** -0.5
    group_size = HQ // KVH
    block_count = length // block_rows
    query_all = queries.reshape(length, KVH, group_size, DH)
    grad_all = grad_out.reshape(length, KVH, group_size, DH)
    out_all = attn_out.reshape(length, KVH, group_size, DH)
    norm_all = jnp.transpose(log_norm, (1, 0, 2)).reshape(KVH, group_size, length)
    starts = doc_start.reshape(length)
    key_all = keys.reshape(length, KVH, DH)
    value_all = values.reshape(length, KVH, DH)
    query_rows = jnp.arange(block_rows, dtype=jnp.int32)[:, None]
    offsets = jnp.arange(3 * block_rows, dtype=jnp.int32)[None, :] - 2 * block_rows

    def per_head(head):
        query_head = query_all[:, head]
        grad_head = grad_all[:, head]
        out_head = out_all[:, head]
        norm_head = norm_all[head]
        front = jnp.zeros((2 * block_rows, DH), keys.dtype)
        key_pad = jnp.concatenate([front, key_all[:, head]], axis=0)
        value_pad = jnp.concatenate([front, value_all[:, head]], axis=0)

        def advance(travel, index):
            key_acc, value_acc = travel
            row_start = index * block_rows
            query_block = lax.dynamic_slice_in_dim(query_head, row_start, block_rows, 0).astype(jnp.float32)
            grad_block = lax.dynamic_slice_in_dim(grad_head, row_start, block_rows, 0).astype(jnp.float32)
            out_block = lax.dynamic_slice_in_dim(out_head, row_start, block_rows, 0).astype(jnp.float32)
            norm_block = lax.dynamic_slice_in_dim(norm_head, row_start, block_rows, 1)
            start_block = lax.dynamic_slice_in_dim(starts, row_start, block_rows, 0)
            key_block = lax.dynamic_slice_in_dim(key_pad, row_start, 3 * block_rows, 0).astype(jnp.float32)
            value_block = lax.dynamic_slice_in_dim(value_pad, row_start, 3 * block_rows, 0).astype(jnp.float32)
            allowed = (offsets <= query_rows) & (offsets > query_rows - window)
            allowed = allowed & (row_start + offsets >= start_block[:, None])
            row_delta = jnp.sum(grad_block * out_block, axis=-1)
            scores = jnp.einsum("qgd,kd->gqk", query_block, key_block) * score_scale
            weights = jnp.where(allowed[None], jnp.exp(scores - norm_block[:, :, None]), 0.0)
            weights_low = lax.optimization_barrier(weights.astype(jnp.bfloat16)).astype(jnp.float32)
            value_part = jnp.einsum("gqk,qgd->kd", weights_low, grad_block)
            grad_weights = jnp.einsum("qgd,kd->gqk", grad_block, value_block)
            dscore = weights * (grad_weights - jnp.transpose(row_delta)[:, :, None])
            dscore_low = lax.optimization_barrier(dscore.astype(jnp.bfloat16)).astype(jnp.float32)
            query_part = jnp.einsum("gqk,kd->qgd", dscore_low, key_block) * score_scale
            key_part = jnp.einsum("gqk,qgd->kd", dscore_low, query_block) * score_scale
            key_acc = lax.dynamic_update_slice_in_dim(
                key_acc, lax.dynamic_slice_in_dim(key_acc, row_start, 3 * block_rows, 0) + key_part, row_start, 0)
            value_acc = lax.dynamic_update_slice_in_dim(
                value_acc, lax.dynamic_slice_in_dim(value_acc, row_start, 3 * block_rows, 0) + value_part, row_start, 0)
            return (key_acc, value_acc), query_part.astype(jnp.bfloat16)

        zeros = jnp.zeros((length + 2 * block_rows, DH), jnp.float32)
        (key_acc, value_acc), query_grads = lax.scan(
            advance, (zeros, zeros), jnp.arange(block_count, dtype=jnp.int32))
        return (query_grads.reshape(length, group_size, DH),
                key_acc[2 * block_rows:].astype(jnp.bfloat16),
                value_acc[2 * block_rows:].astype(jnp.bfloat16))

    query_grads, key_grads, value_grads = lax.map(per_head, jnp.arange(KVH, dtype=jnp.int32))
    grad_queries = jnp.transpose(query_grads, (1, 0, 2, 3)).reshape(length, HQ * DH)
    grad_keys = jnp.transpose(key_grads, (1, 0, 2)).reshape(length, KVH * DH)
    grad_values = jnp.transpose(value_grads, (1, 0, 2)).reshape(length, KVH * DH)
    return grad_queries, grad_keys, grad_values
```

```python
import functools

import jax
import jax.numpy as jnp
from jax import lax
from jax.experimental import pallas as pl
from jax.experimental.pallas import tpu as pltpu
from jax.sharding import PartitionSpec as P

DH = 128
AXES = ("ulysses", "blk")
LOG2E = 1.4426950408889634
BIG = 1e30


def shifted(value, steps):
    count = lax.axis_size("ulysses") * lax.axis_size("blk")
    pairs = [(s, s + steps) for s in range(count) if 0 <= s + steps < count]
    return lax.ppermute(value, AXES, pairs)


def dot(a, b, dims):
    return lax.dot_general(a, b, (dims, ((), ())), preferred_element_type=jnp.float32)


def key_rows(far_ref, near_ref, own_ref):
    return jnp.concatenate([far_ref[...], near_ref[...], own_ref[...]], axis=0)


def mask_bias(base_ref, start_ref, span, tokens):
    far = span - tokens
    key = lax.broadcasted_iota(jnp.int32, (span, tokens), 0) - far
    query = lax.broadcasted_iota(jnp.int32, (span, tokens), 1)
    window = 3 * tokens // 2
    start = start_ref[...] - base_ref[0]
    allowed = (key <= query) & (key > query - window) & (key >= start)
    return jnp.where(allowed, 0.0, -jnp.inf)


def weights_of(keys, q_pair, bias, log_rows):
    scores = dot(keys, q_pair, ((1,), (1,))) * (DH**-0.5 * LOG2E)
    count = len(log_rows)
    shift = jnp.concatenate([bias - LOG2E * row for row in log_rows], axis=1)
    return jnp.exp2(scores + shift)


PAIR = 2


def value_kernel(base_ref, start_ref, q_ref, g_ref, kf_ref, kn_ref, ko_ref, log_ref, far_ref, near_ref, own_ref):
    tokens = q_ref.shape[0]
    heads = q_ref.shape[1] // DH
    keys = key_rows(kf_ref, kn_ref, ko_ref)
    span = keys.shape[0]
    bias = mask_bias(base_ref, start_ref, span, tokens)
    total = None
    for first in range(0, heads, PAIR):
        cut = [slice(h * DH, (h + 1) * DH) for h in range(first, first + PAIR)]
        q_pair = jnp.concatenate([q_ref[:, c] for c in cut], axis=0)
        g_pair = jnp.concatenate([g_ref[:, c] for c in cut], axis=0)
        weights = weights_of(keys, q_pair, bias, [log_ref[h : h + 1, :] for h in range(first, first + PAIR)])
        part = dot(weights.astype(jnp.bfloat16), g_pair, ((1,), (0,)))
        total = part if total is None else total + part
    far = far_ref.shape[0]
    far_ref[...] = total[:far].astype(jnp.bfloat16)
    near_ref[...] = total[far : far + tokens].astype(jnp.bfloat16)
    own_ref[...] = total[far + tokens :]


def key_kernel(base_ref, start_ref, q_ref, g_ref, o_ref, kf_ref, kn_ref, ko_ref, vf_ref, vn_ref, vo_ref, log_ref,
               dq_ref, far_ref, near_ref, own_ref):
    tokens = q_ref.shape[0]
    heads = q_ref.shape[1] // DH
    per = o_ref.shape[2] // DH
    keys = key_rows(kf_ref, kn_ref, ko_ref)
    vals = key_rows(vf_ref, vn_ref, vo_ref)
    span = keys.shape[0]
    vals = jnp.concatenate([vals, jnp.full((span, DH), -1.0, jnp.bfloat16)], axis=1)
    bias = mask_bias(base_ref, start_ref, span, tokens)
    total = None
    for first in range(0, heads, PAIR):
        some = range(first, first + PAIR)
        cut = [slice(h * DH, (h + 1) * DH) for h in some]
        q_pair = jnp.concatenate([q_ref[:, c] for c in cut], axis=0)
        g_pair = jnp.concatenate([g_ref[:, c] for c in cut], axis=0)
        o_pair = jnp.concatenate([o_ref[h // per, :, (h % per) * DH : (h % per + 1) * DH] for h in some], axis=0)
        weights = weights_of(keys, q_pair, bias, [log_ref[h : h + 1, :] for h in some])
        both = jnp.concatenate([g_pair, g_pair * o_pair], axis=1)
        centred = dot(vals, both, ((1,), (1,)))
        dscore = (weights * centred).astype(jnp.bfloat16)
        part = dot(dscore, q_pair, ((1,), (0,)))
        total = part if total is None else total + part
        grad_q = dot(dscore, keys, ((0,), (0,))) * DH**-0.5
        for i, c in enumerate(cut):
            dq_ref[:, c] = grad_q[i * tokens : (i + 1) * tokens].astype(jnp.bfloat16)
    total = total * DH**-0.5
    far = far_ref.shape[0]
    far_ref[...] = total[:far].astype(jnp.bfloat16)
    near_ref[...] = total[far : far + tokens].astype(jnp.bfloat16)
    own_ref[...] = total[far + tokens :]


def body(queries, keys, values, grad_out, attn_out, log_norm, doc_start):
    tokens = queries.shape[0]
    heads = queries.shape[1] // DH
    kv_heads = keys.shape[1] // DH
    group = heads // kv_heads
    ranks = lax.axis_size("ulysses")
    per_rank = group // (heads // ranks)
    far = tokens // 2
    u = lax.axis_index("ulysses")
    place = u * lax.axis_size("blk") + lax.axis_index("blk")
    base = (place * tokens).astype(jnp.int32).reshape(1)
    start = lax.dynamic_slice_in_dim(doc_start, u, 1, 0)

    out_mine = lax.all_to_all(attn_out, "ulysses", split_axis=0, concat_axis=0, tiled=True)
    log_mine = lax.all_to_all(log_norm, "ulysses", split_axis=0, concat_axis=0, tiled=True).reshape(heads, tokens)
    paired = jnp.concatenate([keys, values], axis=1)
    kv_near = shifted(paired, 1)
    kv_far = shifted(paired[tokens - far :], 2)

    smem = pl.BlockSpec(memory_space=pltpu.SMEM)
    whole = lambda shape: pl.BlockSpec(shape, lambda i: (0,) * len(shape))
    cols = lambda rows, width, base=0: pl.BlockSpec((rows, width), lambda i: (0, base + i))
    out_kv = [
        jax.ShapeDtypeStruct((far, kv_heads * DH), jnp.bfloat16),
        jax.ShapeDtypeStruct((tokens, kv_heads * DH), jnp.bfloat16),
        jax.ShapeDtypeStruct((tokens, kv_heads * DH), jnp.float32),
    ]
    out_kv_specs = [cols(far, DH), cols(tokens, DH), cols(tokens, DH)]
    span = 2 * tokens + far
    unit = heads * span * tokens * DH * 2
    params = pltpu.CompilerParams(vmem_limit_bytes=40 * 1024 * 1024)
    log_spec = pl.BlockSpec((group, tokens), lambda i: (i, 0))
    dv_far, dv_near, dv_own = pl.pallas_call(
        value_kernel,
        grid=(kv_heads,),
        in_specs=[smem, whole((1, tokens)), cols(tokens, group * DH), cols(tokens, group * DH),
                  cols(far, DH), cols(tokens, DH), cols(tokens, DH), log_spec],
        out_specs=out_kv_specs,
        out_shape=out_kv,
        compiler_params=params,
        cost_estimate=pl.CostEstimate(flops=4 * unit, bytes_accessed=4 << 20, transcendentals=heads * span * tokens),
        name="value_grads",
    )(base, start, queries, grad_out, kv_far, kv_near, keys, log_mine)
    rv_near = shifted(dv_near, -1)
    rv_far = shifted(dv_far, -2)
    dq, dk_far, dk_near, dk_own = pl.pallas_call(
        key_kernel,
        grid=(kv_heads,),
        in_specs=[smem, whole((1, tokens)), cols(tokens, group * DH), cols(tokens, group * DH),
                  pl.BlockSpec((per_rank, tokens, heads // ranks * DH), lambda i: (i, 0, 0)),
                  cols(far, DH), cols(tokens, DH), cols(tokens, DH),
                  cols(far, DH, kv_heads), cols(tokens, DH, kv_heads), cols(tokens, DH), log_spec],
        out_specs=[cols(tokens, group * DH)] + out_kv_specs,
        out_shape=[jax.ShapeDtypeStruct(queries.shape, jnp.bfloat16)] + out_kv,
        compiler_params=params,
        cost_estimate=pl.CostEstimate(flops=6 * unit, bytes_accessed=6 << 20, transcendentals=heads * span * tokens),
        name="key_grads",
    )(base, start, queries, grad_out, out_mine, kv_far, kv_near, keys, kv_far, kv_near, values, log_mine)
    rk_near = shifted(dk_near, -1)
    rk_far = shifted(dk_far, -2)

    def total(own, near, beyond):
        beyond = jnp.pad(beyond.astype(jnp.float32), ((tokens - far, 0), (0, 0)))
        return (own + near.astype(jnp.float32) + beyond).astype(jnp.bfloat16)

    return dq, total(dk_own, rk_near, rk_far), total(dv_own, rv_near, rv_far)


def solution(mesh):
    return jax.shard_map(
        body,
        mesh=mesh,
        in_specs=(
            P(("ulysses", "blk"), None),
            P(("ulysses", "blk"), None),
            P(("ulysses", "blk"), None),
            P(("ulysses", "blk"), None),
            P(None, "blk", "ulysses"),
            P(None, "ulysses", "blk"),
            P(None, "blk"),
        ),
        out_specs=(
            P(("ulysses", "blk"), None),
            P(("ulysses", "blk"), None),
            P(("ulysses", "blk"), None),
        ),
        check_vma=False,
    )
```

```python
import jax
import jax.numpy as jnp
from jax import lax
from jax.experimental import pallas as pl
from jax.experimental.pallas import tpu as pltpu
from jax.sharding import PartitionSpec as P

DH = 128
AXES = ("ulysses", "blk")
LOG2E = 1.4426950408889634
SCALE = DH**-0.5
RUN = 4
PAD = 16


def shifted(value, steps):
    count = lax.axis_size("ulysses") * lax.axis_size("blk")
    pairs = [(s, s + steps) for s in range(count) if 0 <= s + steps < count]
    return lax.ppermute(value, AXES, pairs)


def routes(steps):
    ranks, blocks = lax.axis_size("ulysses"), lax.axis_size("blk")
    run = min(4, blocks)
    direct, across = [], []
    for source in range(ranks * blocks - steps):
        target = source + steps
        rank, place = divmod(source, blocks)
        if target == (ranks - 2) * blocks:
            direct.append((source, 0))
            across.append((0, target))
        elif place % run + steps == run + steps - 1 and (steps > 1 or target // blocks % 2 == 1):
            middle = (rank if steps > 1 else rank | 1) * blocks + place - run + steps
            direct.append((source, middle))
            across.append((middle, target))
        else:
            direct.append((source, target))
    return direct, across


def passed_on(value, steps):
    direct, across = routes(steps)
    arrived = lax.ppermute(value, AXES, direct)
    return arrived, lax.ppermute(arrived, AXES, across)


def dot(a, b, dims):
    return lax.dot_general(a, b, (dims, ((), ())), preferred_element_type=jnp.float32)


def pair_kernel(k_ref, v_ref, near_ref, far_ref):
    tokens = k_ref.shape[0]
    half = tokens // 2
    near_ref[:tokens] = k_ref[...]
    near_ref[tokens:] = v_ref[...]
    far_ref[:half] = k_ref[half:]
    far_ref[half:] = v_ref[half:]


def pack_kernel(o_ref, log_ref, packed_ref):
    tokens = o_ref.shape[1]
    half = tokens // 2
    packed_ref[:, :tokens] = o_ref[...]
    lane = lax.broadcasted_iota(jnp.int32, (1, tokens), 1)
    for c in range(log_ref.shape[0]):
        rows = []
        for a in range(0, log_ref.shape[1], 2):
            one, two = log_ref[c, a : a + 1, :], log_ref[c, a + 1 : a + 2, :]
            rows.append(jnp.where(lane < half, one, pltpu.roll(two, half, 1)))
            rows.append(jnp.where(lane < half, pltpu.roll(one, half, 1), two))
        left = jnp.concatenate(rows, axis=1)
        terms = []
        for _ in range(3):
            term = left.astype(jnp.bfloat16).astype(jnp.float32)
            left = left - term
            terms.append(term)
        terms.append(jnp.zeros((PAD - 3, left.shape[1]), jnp.float32))
        packed_ref[c, tokens:] = jnp.concatenate(terms, axis=0).astype(jnp.bfloat16)


def head_cols(ref, rows, head):
    return ref[rows, head * DH : (head + 1) * DH]


def stacked_heads(ref, rows, heads):
    return jnp.concatenate([head_cols(ref, rows, h) for h in heads], axis=0)


def out_rows(ref, rows, heads, per):
    return jnp.concatenate([ref[h // per, rows, h % per * DH : (h % per + 1) * DH] for h in heads], axis=0)


def mask_bias(place_ref, start_ref, first_key, first_query, span, half):
    tokens = 2 * half
    key = lax.broadcasted_iota(jnp.int32, (span, tokens), 0) + first_key
    lane = lax.broadcasted_iota(jnp.int32, (span, tokens), 1)
    query = lax.rem(lane, half) + first_query
    start = start_ref[...] - place_ref[0]
    low = lax.broadcasted_iota(jnp.int32, start.shape, 1) < half
    moved = pltpu.roll(start, half, 1)
    start = jnp.where(low, moved, start) if first_query else jnp.where(low, start, moved)
    allowed = (key <= query) & (key > query - 3 * tokens // 2) & (key >= start)
    return jnp.where(allowed, 0.0, -jnp.inf)


def weights_of(keys, q_rows, bias, rows):
    shift = jnp.concatenate([bias - row for row in rows], axis=1)
    return jnp.exp2(dot(keys, q_rows, ((1,), (1,))) * (SCALE * LOG2E) + shift)


def centre_cols(g_rows, o_rows):
    prod = g_rows.astype(jnp.float32) * o_rows.astype(jnp.float32)
    prod = prod + pltpu.roll(prod, DH // 2, 1)
    head = prod.astype(jnp.bfloat16).astype(jnp.float32)
    lane = lax.broadcasted_iota(jnp.int32, prod.shape, 1)
    return jnp.where(lane < DH // 2, head, prod - head).astype(jnp.bfloat16)


def score_grads(weights, vals, g_rows, o_rows):
    vals = jnp.concatenate([vals, jnp.full(vals.shape, -1.0, vals.dtype)], axis=1)
    both = jnp.concatenate([g_rows, centre_cols(g_rows, o_rows)], axis=1)
    return (weights * dot(vals, both, ((1,), (1,)))).astype(jnp.bfloat16)


def key_value_kernel(place_ref, start_ref, q_ref, g_ref, k_own, v_own, far_hbm, far_fixed, near_hbm, near_fixed, packed_hbm,
                     far_out, near_out, dk_own, dv_own, ds_ref, keys_out, far_ref, near_ref, packed_ref, sems):
    tokens, width = q_ref.shape
    half = tokens // 2
    kv_heads = k_own.shape[1] // DH
    group = width // DH // kv_heads
    ranks = packed_ref.shape[0]
    per = width // DH // ranks
    sources = ((far_hbm, far_fixed, far_ref), (near_hbm, near_fixed, near_ref))
    for i, (direct, fixed, target) in enumerate(sources):
        staged = place_ref[1 + i] == 1
        pl.when(staged)(pltpu.make_async_copy(fixed, target, sems.at[i]).start)
        pl.when(jnp.logical_not(staged))(pltpu.make_async_copy(direct, target, sems.at[i]).start)
    moves = []
    for kv in range(kv_heads):
        some = pl.ds(kv * group // per, group // per)
        moves.append((packed_hbm.at[some], packed_ref.at[some]))
    copies = [pltpu.make_async_copy(a, b, sems.at[2 + i]) for i, (a, b) in enumerate(moves)]
    for copy in copies:
        copy.start()
    bias_top = mask_bias(place_ref, start_ref, -3 * half, 0, 4 * half, half)
    bias_low = mask_bias(place_ref, start_ref, -2 * half, half, 4 * half, half)
    top, low = slice(0, half), slice(half, tokens)
    for i, (direct, _, target) in enumerate(sources):
        pltpu.make_async_copy(direct, target, sems.at[i]).wait()
    keys_out[:half] = far_ref[:half]
    keys_out[half:] = near_ref[:tokens]
    for kv in range(kv_heads):
        copies[kv].wait()
        logs = []
        for r in range(kv * group // per, (kv + 1) * group // per):
            terms = packed_ref[r, tokens : tokens + PAD, :].astype(jnp.float32)
            logs.append(LOG2E * (terms[0:1] + terms[1:2] + terms[2:3]))
        cols = slice(kv * DH, (kv + 1) * DH)
        k_near, v_near = near_ref[:tokens, cols], near_ref[tokens:, cols]
        sides = (
            (top, bias_top, jnp.concatenate([far_ref[:half, cols], k_near, k_own[top, cols]], axis=0),
             jnp.concatenate([far_ref[half:, cols], v_near, v_own[top, cols]], axis=0)),
            (low, bias_low, jnp.concatenate([k_near, k_own[:, cols]], axis=0),
             jnp.concatenate([v_near, v_own[:, cols]], axis=0)),
        )
        sums = []
        for side, (rows, bias, keys, vals) in enumerate(sides):
            val_sum = key_sum = 0.0
            for first in range(kv * group, (kv + 1) * group, RUN):
                heads = range(first, first + RUN)
                shifts = []
                for h in heads[::2]:
                    at = (h % per + side) * DH
                    shifts.append(logs[h // per - kv * group // per][:, at : at + DH])
                q_rows, g_rows = stacked_heads(q_ref, rows, heads), stacked_heads(g_ref, rows, heads)
                weights = weights_of(keys, q_rows, bias, shifts)
                val_sum += dot(weights.astype(jnp.bfloat16), g_rows, ((1,), (0,)))
                dscore = score_grads(weights, vals, g_rows, out_rows(packed_ref, rows, heads, per))
                key_sum += dot(dscore, q_rows, ((1,), (0,)))
                at = (side * width // DH + first) * half
                ds_ref[:, at : at + RUN * half] = dscore
            sums.append((key_sum * SCALE, val_sum))
        for i, own in enumerate((dk_own, dv_own)):
            one, two = sums[0][i], sums[1][i]
            far_out[i * half : (i + 1) * half, cols] = one[:half].astype(jnp.bfloat16)
            near_out[i * tokens : (i + 1) * tokens, cols] = (one[half : 3 * half] + two[:tokens]).astype(jnp.bfloat16)
            own[top, cols] = one[3 * half :] + two[tokens : tokens + half]
            own[low, cols] = two[tokens + half :]


def query_kernel(halo_ref, k_own, ds_ref, dq_ref):
    tokens, width = dq_ref.shape
    half = tokens // 2
    kv_heads = k_own.shape[1] // DH
    group = width // DH // kv_heads
    for kv in range(kv_heads):
        cols = slice(kv * DH, (kv + 1) * DH)
        sides = (
            jnp.concatenate([halo_ref[:, cols], k_own[:half, cols]], axis=0),
            jnp.concatenate([halo_ref[half:, cols], k_own[:, cols]], axis=0),
        )
        for side, keys in enumerate(sides):
            for first in range(kv * group, (kv + 1) * group, RUN):
                at = (side * width // DH + first) * half
                grad_q = (dot(ds_ref[:, at : at + RUN * half], keys, ((0,), (0,))) * SCALE).astype(jnp.bfloat16)
                for i in range(RUN):
                    out = slice((first + i) * DH, (first + i + 1) * DH)
                    dq_ref[side * half : (side + 1) * half, out] = grad_q[i * half : (i + 1) * half]


def call(kernel, name, outs, *args, flops, in_hbm=(), out_hbm=0, scratch=(), limit=24):
    smem = pl.BlockSpec(memory_space=pltpu.SMEM)
    vmem = pl.BlockSpec(memory_space=pltpu.VMEM)
    hbm = pl.BlockSpec(memory_space=pl.ANY)
    return pl.pallas_call(
        kernel,
        in_specs=[smem if a.ndim == 1 else vmem for a in args] + [hbm] * len(in_hbm),
        out_specs=[vmem] * (len(outs) - out_hbm) + [hbm] * out_hbm,
        out_shape=[jax.ShapeDtypeStruct(s, d) for s, d in outs],
        compiler_params=pltpu.CompilerParams(vmem_limit_bytes=limit * 1024 * 1024),
        cost_estimate=pl.CostEstimate(flops=flops, bytes_accessed=4 << 20, transcendentals=1 << 20),
        scratch_shapes=scratch,
        name=name,
    )(*args, *in_hbm)


def body(queries, keys, values, grad_out, attn_out, log_norm, doc_start):
    tokens, width = queries.shape
    kv_width = keys.shape[1]
    half = tokens // 2
    heads = width // DH
    ranks = lax.axis_size("ulysses")
    rank = lax.axis_index("ulysses")
    index = rank * lax.axis_size("blk") + lax.axis_index("blk")
    run_place = index % min(4, lax.axis_size("blk"))
    beyond = index - (ranks - 2) * lax.axis_size("blk")
    far_turns = (run_place == 1) | (beyond == 0)
    near_turns = ((run_place == 0) & (rank % 2 == 1)) | (beyond == 0)
    place = jnp.stack([index * tokens, far_turns, near_turns]).astype(jnp.int32)
    start = lax.dynamic_slice_in_dim(doc_start, rank, 1, 0)
    bf16, f32 = jnp.bfloat16, jnp.float32

    wide, both = (tokens, kv_width), (2 * tokens, kv_width)
    near, far = call(pair_kernel, "pair", [(both, bf16), (wide, bf16)], keys, values, flops=0)
    near, near_fixed = passed_on(near, 1)
    far, far_fixed = passed_on(far, 2)
    rank_width = attn_out.shape[2]
    step = ranks // 4
    block = lambda *shape: pl.BlockSpec((step,) + shape, lambda c: (c, 0, 0))
    packed = pl.pallas_call(
        pack_kernel,
        grid=(ranks // step,),
        in_specs=[block(tokens, rank_width), block(heads // ranks, tokens)],
        out_specs=block(tokens + PAD, rank_width),
        out_shape=jax.ShapeDtypeStruct((ranks, tokens + PAD, rank_width), bf16),
        name="pack",
    )(attn_out, log_norm)
    packed = lax.all_to_all(packed, "ulysses", split_axis=0, concat_axis=0, tiled=True)

    unit = 2 * heads * 8 * half * half * DH
    r_far, r_near, dk_own, dv_own, dscore, key_halo = call(
        key_value_kernel, "key_value_grads",
        [(wide, bf16), (both, bf16), (wide, f32), (wide, f32), ((4 * half, 2 * heads * half), bf16),
         ((3 * half, kv_width), bf16)],
        place, start, queries, grad_out, keys, values, in_hbm=(far, far_fixed, near, near_fixed, packed), flops=4 * unit,
        scratch=[pltpu.VMEM(wide, bf16), pltpu.VMEM(both, bf16), pltpu.VMEM(packed.shape, bf16),
                 pltpu.SemaphoreType.DMA((2 + kv_width // DH,))])
    r_far = shifted(r_far, -2)
    r_near = shifted(r_near, -1)
    (grad_queries,) = call(query_kernel, "query_grads", [(queries.shape, bf16)], key_halo, keys, dscore, flops=unit)

    def total(own, near_part, far_part):
        far_part = jnp.pad(far_part.astype(f32), ((half, 0), (0, 0)))
        return (own + near_part.astype(f32) + far_part).astype(bf16)

    return (grad_queries, total(dk_own, r_near[:tokens], r_far[:half]), total(dv_own, r_near[tokens:], r_far[half:]))


def solution(mesh):
    tokens_spec = P(AXES, None)
    return jax.shard_map(
        body,
        mesh=mesh,
        in_specs=(tokens_spec,) * 4 + (P(None, "blk", "ulysses"), P(None, "ulysses", "blk"), P(None, "blk")),
        out_specs=(tokens_spec,) * 3,
        check_vma=False,
    )
```

```python
import jax
import jax.numpy as jnp
from jax import lax
from jax.experimental import pallas as pl
from jax.experimental.pallas import tpu as pltpu
from jax.sharding import PartitionSpec as P

DH = 128
AXES = ("ulysses", "blk")
LOG2E = 1.4426950408889634
SCALE = DH**-0.5
RUN = 4
PAD = 16


def shifted(value, steps):
    count = lax.axis_size("ulysses") * lax.axis_size("blk")
    pairs = [(s, s + steps) for s in range(count) if 0 <= s + steps < count]
    return lax.ppermute(value, AXES, pairs)


def routes(steps):
    ranks, blocks = lax.axis_size("ulysses"), lax.axis_size("blk")
    run = min(4, blocks)
    direct, across = [], []
    for source in range(ranks * blocks - steps):
        target = source + steps
        rank, place = divmod(source, blocks)
        if target == (ranks - 2) * blocks:
            direct.append((source, 0))
            across.append((0, target))
        elif place % run + steps == run + steps - 1 and (steps > 1 or target // blocks % 2 == 1):
            middle = (rank if steps > 1 else rank | 1) * blocks + place - run + steps
            direct.append((source, middle))
            across.append((middle, target))
        else:
            direct.append((source, target))
    return direct, across


def passed_on(value, steps):
    direct, across = routes(steps)
    arrived = lax.ppermute(value, AXES, direct)
    return arrived, lax.ppermute(arrived, AXES, across)


def dot(a, b, dims):
    return lax.dot_general(a, b, (dims, ((), ())), preferred_element_type=jnp.float32)


def pair_kernel(k_ref, v_ref, near_ref, far_ref):
    tokens = k_ref.shape[0]
    half = tokens // 2
    near_ref[:tokens] = k_ref[...]
    near_ref[tokens:] = v_ref[...]
    far_ref[:half] = k_ref[half:]
    far_ref[half:] = v_ref[half:]


def pack_kernel(log_ref, o_hbm, packed_hbm, packed, sems):
    count, per, tokens = log_ref.shape
    half = tokens // 2
    loads = [pltpu.make_async_copy(o_hbm.at[c], packed.at[c, pl.ds(0, tokens)], sems.at[0, c]) for c in range(count)]
    stores = [pltpu.make_async_copy(packed.at[c], packed_hbm.at[c], sems.at[1, c]) for c in range(count)]
    for load in loads:
        load.start()
    lane = lax.broadcasted_iota(jnp.int32, (1, tokens), 1)
    for c in range(count):
        rows = []
        for a in range(0, per, 2):
            one, two = log_ref[c, a : a + 1, :], log_ref[c, a + 1 : a + 2, :]
            rows.append(jnp.where(lane < half, one, pltpu.roll(two, half, 1)))
            rows.append(jnp.where(lane < half, pltpu.roll(one, half, 1), two))
        left = jnp.concatenate(rows, axis=1)
        terms = []
        for _ in range(3):
            term = left.astype(jnp.bfloat16).astype(jnp.float32)
            left = left - term
            terms.append(term)
        terms.append(jnp.zeros((PAD - 3, left.shape[1]), jnp.float32))
        packed[c, tokens:] = jnp.concatenate(terms, axis=0).astype(jnp.bfloat16)
        loads[c].wait()
        stores[c].start()
    for store in stores:
        store.wait()


def head_cols(ref, rows, head):
    return ref[rows, head * DH : (head + 1) * DH]


def stacked_heads(ref, rows, heads):
    return jnp.concatenate([head_cols(ref, rows, h) for h in heads], axis=0)


def out_rows(ref, rows, heads, per):
    return jnp.concatenate([ref[h // per, rows, h % per * DH : (h % per + 1) * DH] for h in heads], axis=0)


def mask_bias(place_ref, start_ref, first_key, first_query, span, half):
    tokens = 2 * half
    key = lax.broadcasted_iota(jnp.int32, (span, tokens), 0) + first_key
    lane = lax.broadcasted_iota(jnp.int32, (span, tokens), 1)
    query = lax.rem(lane, half) + first_query
    start = start_ref[...] - place_ref[0]
    low = lax.broadcasted_iota(jnp.int32, start.shape, 1) < half
    moved = pltpu.roll(start, half, 1)
    start = jnp.where(low, moved, start) if first_query else jnp.where(low, start, moved)
    allowed = (key <= query) & (key > query - 3 * tokens // 2) & (key >= start)
    return jnp.where(allowed, 0.0, -jnp.inf)


def weights_of(keys, q_rows, bias, rows):
    shift = jnp.concatenate([bias - row for row in rows], axis=1)
    return jnp.exp2(dot(keys, q_rows, ((1,), (1,))) * (SCALE * LOG2E) + shift)


def centre_cols(g_rows, o_rows):
    prod = g_rows.astype(jnp.float32) * o_rows.astype(jnp.float32)
    prod = prod + pltpu.roll(prod, DH // 2, 1)
    head = prod.astype(jnp.bfloat16).astype(jnp.float32)
    lane = lax.broadcasted_iota(jnp.int32, prod.shape, 1)
    return jnp.where(lane < DH // 2, head, prod - head).astype(jnp.bfloat16)


def score_grads(weights, vals, g_rows, o_rows):
    vals = jnp.concatenate([vals, jnp.full(vals.shape, -1.0, vals.dtype)], axis=1)
    both = jnp.concatenate([g_rows, centre_cols(g_rows, o_rows)], axis=1)
    return (weights * dot(vals, both, ((1,), (1,)))).astype(jnp.bfloat16)


def log_terms(packed_ref, ranks, tokens):
    logs = {}
    for r in ranks:
        terms = packed_ref[r, tokens : tokens + PAD, :].astype(jnp.float32)
        logs[r] = LOG2E * (terms[0:1] + terms[1:2] + terms[2:3])
    return logs


def run_grads(q_ref, g_ref, packed_ref, logs, side, heads, per, keys, vals, bias):
    half = q_ref.shape[0] // 2
    rows = slice(side * half, (side + 1) * half)
    shifts = []
    for h in heads[::2]:
        at = (h % per + side) * DH
        shifts.append(logs[h // per][:, at : at + DH])
    q_rows, g_rows = stacked_heads(q_ref, rows, heads), stacked_heads(g_ref, rows, heads)
    weights = weights_of(keys, q_rows, bias, shifts)
    dscore = score_grads(weights, vals, g_rows, out_rows(packed_ref, rows, heads, per))
    return weights.astype(jnp.bfloat16), dscore, q_rows, g_rows


def start_all(pairs, sems, first):
    copies = [pltpu.make_async_copy(a, b, sems.at[first + i]) for i, (a, b) in enumerate(pairs)]
    for copy in copies:
        copy.start()
    return copies


def packed_moves(packed_hbm, packed_ref, kv_heads):
    ranks = packed_ref.shape[0] // kv_heads
    return [(packed_hbm.at[pl.ds(kv * ranks, ranks)], packed_ref.at[pl.ds(kv * ranks, ranks)]) for kv in range(kv_heads)]


def halo_kernel(place_ref, start_ref, q_ref, g_ref, far_hbm, far_fixed, near_hbm, near_fixed, packed_hbm,
                far_out, near_out, keys_out, ds_top, ds_low, far_ref, near_ref, packed_ref, sems):
    tokens, width = q_ref.shape
    half = tokens // 2
    kv_heads = far_ref.shape[1] // DH
    group = width // DH // kv_heads
    per = width // DH // packed_ref.shape[0]
    sources = ((far_hbm, far_fixed, far_ref), (near_hbm, near_fixed, near_ref))
    for i, (direct, fixed, target) in enumerate(sources):
        staged = place_ref[1 + i] == 1
        pl.when(staged)(pltpu.make_async_copy(fixed, target, sems.at[i]).start)
        pl.when(jnp.logical_not(staged))(pltpu.make_async_copy(direct, target, sems.at[i]).start)
    copies = start_all(packed_moves(packed_hbm, packed_ref, kv_heads), sems, 2)
    biases = (mask_bias(place_ref, start_ref, -3 * half, 0, 3 * half, half),
              mask_bias(place_ref, start_ref, -2 * half, half, tokens, half))
    for i, (direct, _, target) in enumerate(sources):
        pltpu.make_async_copy(direct, target, sems.at[i]).wait()
    keys_out[:half] = far_ref[:half]
    keys_out[half:] = near_ref[:tokens]
    for kv in range(kv_heads):
        copies[kv].wait()
        logs = log_terms(packed_ref, range(kv * group // per, (kv + 1) * group // per), tokens)
        cols = slice(kv * DH, (kv + 1) * DH)
        k_near, v_near = near_ref[:tokens, cols], near_ref[tokens:, cols]
        keys = (jnp.concatenate([far_ref[:half, cols], k_near], axis=0), k_near)
        vals = (jnp.concatenate([far_ref[half:, cols], v_near], axis=0), v_near)
        sums = []
        for side, ds_ref in enumerate((ds_top, ds_low)):
            val_sum = key_sum = 0.0
            for first in range(kv * group, (kv + 1) * group, RUN):
                weights, dscore, q_rows, g_rows = run_grads(
                    q_ref, g_ref, packed_ref, logs, side, range(first, first + RUN), per, keys[side], vals[side], biases[side])
                val_sum += dot(weights, g_rows, ((1,), (0,)))
                key_sum += dot(dscore, q_rows, ((1,), (0,)))
                ds_ref[:, first * half : (first + RUN) * half] = dscore
            sums.append((key_sum * SCALE, val_sum))
        for i in range(2):
            one, two = sums[0][i], sums[1][i]
            far_out[i * half : (i + 1) * half, cols] = one[:half].astype(jnp.bfloat16)
            near_out[i * tokens : (i + 1) * tokens, cols] = (one[half:] + two).astype(jnp.bfloat16)


def own_kernel(place_ref, start_ref, q_ref, g_ref, k_own, v_own, halo_ref, ds_top, ds_low, packed_hbm,
               dk_own, dv_own, dq_ref, packed_ref, sems):
    tokens, width = q_ref.shape
    half = tokens // 2
    kv_heads = k_own.shape[1] // DH
    group = width // DH // kv_heads
    per = width // DH // packed_ref.shape[0]
    copies = start_all(packed_moves(packed_hbm, packed_ref, kv_heads), sems, 0)
    biases = (mask_bias(place_ref, start_ref, 0, 0, half, half), mask_bias(place_ref, start_ref, 0, half, tokens, half))
    for kv in range(kv_heads):
        copies[kv].wait()
        logs = log_terms(packed_ref, range(kv * group // per, (kv + 1) * group // per), tokens)
        cols = slice(kv * DH, (kv + 1) * DH)
        sums = []
        for side, ds_ref in enumerate((ds_top, ds_low)):
            keys, vals = k_own[: (side + 1) * half, cols], v_own[: (side + 1) * half, cols]
            all_keys = jnp.concatenate([halo_ref[side * half :, cols], keys], axis=0)
            val_sum = key_sum = 0.0
            for first in range(kv * group, (kv + 1) * group, RUN):
                weights, dscore, q_rows, g_rows = run_grads(
                    q_ref, g_ref, packed_ref, logs, side, range(first, first + RUN), per, keys, vals, biases[side])
                val_sum += dot(weights, g_rows, ((1,), (0,)))
                key_sum += dot(dscore, q_rows, ((1,), (0,)))
                dscore = jnp.concatenate([ds_ref[:, first * half : (first + RUN) * half], dscore], axis=0)
                grad_q = (dot(dscore, all_keys, ((0,), (0,))) * SCALE).astype(jnp.bfloat16)
                for i in range(RUN):
                    out = slice((first + i) * DH, (first + i + 1) * DH)
                    dq_ref[side * half : (side + 1) * half, out] = grad_q[i * half : (i + 1) * half]
            sums.append((key_sum * SCALE, val_sum))
        for i, own in enumerate((dk_own, dv_own)):
            one, two = sums[0][i], sums[1][i]
            own[:half, cols] = one + two[:half]
            own[half:, cols] = two[half:]


def call(kernel, name, outs, *args, flops, in_hbm=(), out_hbm=0, scratch=(), limit=24):
    smem = pl.BlockSpec(memory_space=pltpu.SMEM)
    vmem = pl.BlockSpec(memory_space=pltpu.VMEM)
    hbm = pl.BlockSpec(memory_space=pl.ANY)
    return pl.pallas_call(
        kernel,
        in_specs=[smem if a.ndim == 1 else vmem for a in args] + [hbm] * len(in_hbm),
        out_specs=[vmem] * (len(outs) - out_hbm) + [hbm] * out_hbm,
        out_shape=[jax.ShapeDtypeStruct(s, d) for s, d in outs],
        compiler_params=pltpu.CompilerParams(vmem_limit_bytes=limit * 1024 * 1024),
        cost_estimate=pl.CostEstimate(flops=flops, bytes_accessed=4 << 20, transcendentals=1 << 20),
        scratch_shapes=scratch,
        name=name,
    )(*args, *in_hbm)


def body(queries, keys, values, grad_out, attn_out, log_norm, doc_start):
    tokens, width = queries.shape
    kv_width = keys.shape[1]
    half = tokens // 2
    heads = width // DH
    ranks = lax.axis_size("ulysses")
    rank = lax.axis_index("ulysses")
    index = rank * lax.axis_size("blk") + lax.axis_index("blk")
    run_place = index % min(4, lax.axis_size("blk"))
    beyond = index - (ranks - 2) * lax.axis_size("blk")
    far_turns = (run_place == 1) | (beyond == 0)
    near_turns = ((run_place == 0) & (rank % 2 == 1)) | (beyond == 0)
    place = jnp.stack([index * tokens, far_turns, near_turns]).astype(jnp.int32)
    start = lax.dynamic_slice_in_dim(doc_start, rank, 1, 0)
    bf16, f32 = jnp.bfloat16, jnp.float32

    wide, both = (tokens, kv_width), (2 * tokens, kv_width)
    near, far = call(pair_kernel, "pair", [(both, bf16), (wide, bf16)], keys, values, flops=0)
    near, near_fixed = passed_on(near, 1)
    far, far_fixed = passed_on(far, 2)
    sent = (ranks, tokens + PAD, attn_out.shape[2])
    (packed,) = call(
        pack_kernel, "pack", [(sent, bf16)], log_norm, in_hbm=(attn_out,), out_hbm=1, flops=0, limit=60,
        scratch=[pltpu.VMEM(sent, bf16), pltpu.SemaphoreType.DMA((2, ranks))])
    packed = lax.all_to_all(packed, "ulysses", split_axis=0, concat_axis=0, tiled=True)

    unit = 2 * heads * 8 * half * half * DH
    packed_scratch = [pltpu.VMEM(packed.shape, bf16), pltpu.SemaphoreType.DMA((2 + kv_width // DH,))]
    r_far, r_near, key_halo, ds_top, ds_low = call(
        halo_kernel, "halo_grads",
        [(wide, bf16), (both, bf16), ((3 * half, kv_width), bf16), ((3 * half, heads * half), bf16),
         ((tokens, heads * half), bf16)],
        place, start, queries, grad_out, in_hbm=(far, far_fixed, near, near_fixed, packed), flops=3 * unit,
        scratch=[pltpu.VMEM(wide, bf16), pltpu.VMEM(both, bf16)] + packed_scratch)
    r_far = shifted(r_far, -2)
    r_near = shifted(r_near, -1)
    dk_own, dv_own, grad_queries = call(
        own_kernel, "own_grads", [(wide, f32), (wide, f32), (queries.shape, bf16)],
        place, start, queries, grad_out, keys, values, key_halo, ds_top, ds_low, in_hbm=(packed,), flops=3 * unit,
        scratch=packed_scratch)
    r_far = r_far.astype(f32)

    def total(own, near_part, far_part):
        return (own + near_part.astype(f32) + jnp.pad(far_part, ((half, 0), (0, 0)))).astype(bf16)

    return (grad_queries, total(dk_own, r_near[:tokens], r_far[:half]), total(dv_own, r_near[tokens:], r_far[half:]))


def solution(mesh):
    tokens_spec = P(AXES, None)
    return jax.shard_map(
        body,
        mesh=mesh,
        in_specs=(tokens_spec,) * 4 + (P(None, "blk", "ulysses"), P(None, "ulysses", "blk"), P(None, "blk")),
        out_specs=(tokens_spec,) * 3,
        check_vma=False,
    )
```

```python
import jax
import jax.numpy as jnp
from jax import lax
from jax.experimental import pallas as pl
from jax.experimental.pallas import tpu as pltpu
from jax.sharding import PartitionSpec as P

DH = 128
AXES = ("ulysses", "blk")
LOG2E = 1.4426950408889634
SCALE = DH**-0.5
RUN = 4
PAD = 16


def shifted(value, steps):
    count = lax.axis_size("ulysses") * lax.axis_size("blk")
    pairs = [(s, s + steps) for s in range(count) if 0 <= s + steps < count]
    return lax.ppermute(value, AXES, pairs)


def routes(steps):
    ranks, blocks = lax.axis_size("ulysses"), lax.axis_size("blk")
    run = min(4, blocks)
    direct, across = [], []
    for source in range(ranks * blocks - steps):
        target = source + steps
        rank, place = divmod(source, blocks)
        if target == (ranks - 2) * blocks:
            direct.append((source, 0))
            across.append((0, target))
        elif place % run + steps == run + steps - 1 and (steps > 1 or target // blocks % 2 == 1):
            middle = (rank if steps > 1 else rank | 1) * blocks + place - run + steps
            direct.append((source, middle))
            across.append((middle, target))
        else:
            direct.append((source, target))
    return direct, across


def passed_on(value, steps):
    direct, across = routes(steps)
    arrived = lax.ppermute(value, AXES, direct)
    return arrived, lax.ppermute(arrived, AXES, across)


def dot(a, b, dims):
    return lax.dot_general(a, b, (dims, ((), ())), preferred_element_type=jnp.float32)


def pair_kernel(k_ref, v_ref, near_ref, far_ref):
    tokens = k_ref.shape[0]
    half = tokens // 2
    near_ref[:tokens] = k_ref[...]
    near_ref[tokens:] = v_ref[...]
    far_ref[:half] = k_ref[half:]
    far_ref[half:] = v_ref[half:]


def pack_kernel(log_ref, o_hbm, packed_hbm, packed, sems):
    count, per, tokens = log_ref.shape
    half = tokens // 2
    loads = [pltpu.make_async_copy(o_hbm.at[c], packed.at[c, pl.ds(0, tokens)], sems.at[0, c]) for c in range(count)]
    stores = [pltpu.make_async_copy(packed.at[c], packed_hbm.at[c], sems.at[1, c]) for c in range(count)]
    for load in loads:
        load.start()
    lane = lax.broadcasted_iota(jnp.int32, (1, tokens), 1)
    for c in range(count):
        rows = []
        for a in range(0, per, 2):
            one, two = log_ref[c, a : a + 1, :], log_ref[c, a + 1 : a + 2, :]
            rows.append(jnp.where(lane < half, one, pltpu.roll(two, half, 1)))
            rows.append(jnp.where(lane < half, pltpu.roll(one, half, 1), two))
        left = jnp.concatenate(rows, axis=1)
        terms = []
        for _ in range(3):
            term = left.astype(jnp.bfloat16).astype(jnp.float32)
            left = left - term
            terms.append(term)
        terms.append(jnp.zeros((PAD - 3, left.shape[1]), jnp.float32))
        packed[c, tokens:] = jnp.concatenate(terms, axis=0).astype(jnp.bfloat16)
        loads[c].wait()
        stores[c].start()
    for store in stores:
        store.wait()


def head_cols(ref, rows, head):
    return ref[rows, head * DH : (head + 1) * DH]


def stacked_heads(ref, rows, heads):
    return jnp.concatenate([head_cols(ref, rows, h) for h in heads], axis=0)


def out_rows(ref, rows, heads, per):
    return jnp.concatenate([ref[h // per, rows, h % per * DH : (h % per + 1) * DH] for h in heads], axis=0)


def mask_bias(place_ref, start_ref, first_key, first_query, span, half):
    tokens = 2 * half
    key = lax.broadcasted_iota(jnp.int32, (span, tokens), 0) + first_key
    lane = lax.broadcasted_iota(jnp.int32, (span, tokens), 1)
    query = lax.rem(lane, half) + first_query
    start = start_ref[...] - place_ref[0]
    low = lax.broadcasted_iota(jnp.int32, start.shape, 1) < half
    moved = pltpu.roll(start, half, 1)
    start = jnp.where(low, moved, start) if first_query else jnp.where(low, start, moved)
    allowed = (key <= query) & (key > query - 3 * tokens // 2) & (key >= start)
    return jnp.where(allowed, 0.0, -jnp.inf)


def weights_of(keys, q_rows, bias, rows):
    shift = jnp.concatenate([bias - row for row in rows], axis=1)
    return jnp.exp2(dot(keys, q_rows, ((1,), (1,))) * (SCALE * LOG2E) + shift)


def centre_cols(g_rows, o_rows):
    prod = g_rows.astype(jnp.float32) * o_rows.astype(jnp.float32)
    prod = prod + pltpu.roll(prod, DH // 2, 1)
    head = prod.astype(jnp.bfloat16).astype(jnp.float32)
    lane = lax.broadcasted_iota(jnp.int32, prod.shape, 1)
    return jnp.where(lane < DH // 2, head, prod - head).astype(jnp.bfloat16)


def score_grads(weights, vals, g_rows, o_rows):
    vals = jnp.concatenate([vals, jnp.full(vals.shape, -1.0, vals.dtype)], axis=1)
    both = jnp.concatenate([g_rows, centre_cols(g_rows, o_rows)], axis=1)
    return (weights * dot(vals, both, ((1,), (1,)))).astype(jnp.bfloat16)


def log_terms(packed_ref, ranks, tokens):
    logs = {}
    for r in ranks:
        terms = packed_ref[r, tokens : tokens + PAD, :].astype(jnp.float32)
        logs[r] = LOG2E * (terms[0:1] + terms[1:2] + terms[2:3])
    return logs


def run_grads(q_ref, g_ref, packed_ref, logs, side, heads, per, keys, vals, bias):
    half = q_ref.shape[0] // 2
    rows = slice(side * half, (side + 1) * half)
    shifts = []
    for h in heads[::2]:
        at = (h % per + side) * DH
        shifts.append(logs[h // per][:, at : at + DH])
    q_rows, g_rows = stacked_heads(q_ref, rows, heads), stacked_heads(g_ref, rows, heads)
    weights = weights_of(keys, q_rows, bias, shifts)
    dscore = score_grads(weights, vals, g_rows, out_rows(packed_ref, rows, heads, per))
    return weights.astype(jnp.bfloat16), dscore, q_rows, g_rows


def start_all(pairs, sems, first):
    copies = [pltpu.make_async_copy(a, b, sems.at[first + i]) for i, (a, b) in enumerate(pairs)]
    for copy in copies:
        copy.start()
    return copies


def packed_moves(packed_hbm, packed_ref, kv_heads):
    ranks = packed_ref.shape[0] // kv_heads
    return [(packed_hbm.at[pl.ds(kv * ranks, ranks)], packed_ref.at[pl.ds(kv * ranks, ranks)]) for kv in range(kv_heads)]


def halo_kernel(place_ref, start_ref, q_ref, g_ref, far_hbm, far_fixed, near_hbm, near_fixed, packed_hbm,
                far_out, near_out, keys_out, ds_top, ds_low, far_ref, near_ref, packed_ref, sems):
    tokens, width = q_ref.shape
    half = tokens // 2
    kv_heads = far_ref.shape[1] // DH
    group = width // DH // kv_heads
    per = width // DH // packed_ref.shape[0]
    sources = ((far_hbm, far_fixed, far_ref), (near_hbm, near_fixed, near_ref))
    for i, (direct, fixed, target) in enumerate(sources):
        staged = place_ref[1 + i] == 1
        pl.when(staged)(pltpu.make_async_copy(fixed, target, sems.at[i]).start)
        pl.when(jnp.logical_not(staged))(pltpu.make_async_copy(direct, target, sems.at[i]).start)
    copies = start_all(packed_moves(packed_hbm, packed_ref, kv_heads), sems, 2)
    biases = (mask_bias(place_ref, start_ref, -3 * half, 0, 3 * half, half),
              mask_bias(place_ref, start_ref, -2 * half, half, tokens, half))
    for i, (direct, _, target) in enumerate(sources):
        pltpu.make_async_copy(direct, target, sems.at[i]).wait()
    keys_out[:half] = far_ref[:half]
    keys_out[half:] = near_ref[:tokens]
    for kv in range(kv_heads):
        copies[kv].wait()
        logs = log_terms(packed_ref, range(kv * group // per, (kv + 1) * group // per), tokens)
        cols = slice(kv * DH, (kv + 1) * DH)
        k_near, v_near = near_ref[:tokens, cols], near_ref[tokens:, cols]
        keys = (jnp.concatenate([far_ref[:half, cols], k_near], axis=0), k_near)
        vals = (jnp.concatenate([far_ref[half:, cols], v_near], axis=0), v_near)
        sums = []
        for side, ds_ref in enumerate((ds_top, ds_low)):
            val_sum = key_sum = 0.0
            for first in range(kv * group, (kv + 1) * group, RUN):
                weights, dscore, q_rows, g_rows = run_grads(
                    q_ref, g_ref, packed_ref, logs, side, range(first, first + RUN), per, keys[side], vals[side], biases[side])
                val_sum += dot(weights, g_rows, ((1,), (0,)))
                key_sum += dot(dscore, q_rows, ((1,), (0,)))
                ds_ref[:, first * half : (first + RUN) * half] = dscore
            sums.append((key_sum * SCALE, val_sum))
        for i in range(2):
            one, two = sums[0][i], sums[1][i]
            far_out[i * half : (i + 1) * half, cols] = one[:half].astype(jnp.bfloat16)
            near_out[i * tokens : (i + 1) * tokens, cols] = (one[half:] + two).astype(jnp.bfloat16)


def own_kernel(place_ref, start_ref, q_ref, g_ref, k_own, v_own, halo_ref, ds_top, ds_low, packed_hbm,
               dk_own, dv_own, dq_ref, packed_ref, sems):
    tokens, width = q_ref.shape
    half = tokens // 2
    kv_heads = k_own.shape[1] // DH
    group = width // DH // kv_heads
    per = width // DH // packed_ref.shape[0]
    copies = start_all(packed_moves(packed_hbm, packed_ref, kv_heads), sems, 0)
    biases = (mask_bias(place_ref, start_ref, 0, 0, half, half), mask_bias(place_ref, start_ref, 0, half, tokens, half))
    for kv in range(kv_heads):
        copies[kv].wait()
        logs = log_terms(packed_ref, range(kv * group // per, (kv + 1) * group // per), tokens)
        cols = slice(kv * DH, (kv + 1) * DH)
        sums = []
        for side, ds_ref in enumerate((ds_top, ds_low)):
            keys, vals = k_own[: (side + 1) * half, cols], v_own[: (side + 1) * half, cols]
            all_keys = jnp.concatenate([halo_ref[side * half :, cols], keys], axis=0)
            val_sum = key_sum = 0.0
            for first in range(kv * group, (kv + 1) * group, RUN):
                weights, dscore, q_rows, g_rows = run_grads(
                    q_ref, g_ref, packed_ref, logs, side, range(first, first + RUN), per, keys, vals, biases[side])
                val_sum += dot(weights, g_rows, ((1,), (0,)))
                key_sum += dot(dscore, q_rows, ((1,), (0,)))
                dscore = jnp.concatenate([ds_ref[:, first * half : (first + RUN) * half], dscore], axis=0)
                grad_q = (dot(dscore, all_keys, ((0,), (0,))) * SCALE).astype(jnp.bfloat16)
                for i in range(RUN):
                    out = slice((first + i) * DH, (first + i + 1) * DH)
                    dq_ref[side * half : (side + 1) * half, out] = grad_q[i * half : (i + 1) * half]
            sums.append((key_sum * SCALE, val_sum))
        for i, own in enumerate((dk_own, dv_own)):
            one, two = sums[0][i], sums[1][i]
            own[:half, cols] = one + two[:half]
            own[half:, cols] = two[half:]


def call(kernel, name, outs, *args, flops, in_hbm=(), out_hbm=0, scratch=(), limit=24):
    smem = pl.BlockSpec(memory_space=pltpu.SMEM)
    vmem = pl.BlockSpec(memory_space=pltpu.VMEM)
    hbm = pl.BlockSpec(memory_space=pl.ANY)
    return pl.pallas_call(
        kernel,
        in_specs=[smem if a.ndim == 1 else vmem for a in args] + [hbm] * len(in_hbm),
        out_specs=[vmem] * (len(outs) - out_hbm) + [hbm] * out_hbm,
        out_shape=[jax.ShapeDtypeStruct(s, d) for s, d in outs],
        compiler_params=pltpu.CompilerParams(vmem_limit_bytes=limit * 1024 * 1024),
        cost_estimate=pl.CostEstimate(flops=flops, bytes_accessed=4 << 20, transcendentals=1 << 20),
        scratch_shapes=scratch,
        name=name,
    )(*args, *in_hbm)


def body(queries, keys, values, grad_out, attn_out, log_norm, doc_start):
    tokens, width = queries.shape
    kv_width = keys.shape[1]
    half = tokens // 2
    heads = width // DH
    ranks = lax.axis_size("ulysses")
    rank = lax.axis_index("ulysses")
    index = rank * lax.axis_size("blk") + lax.axis_index("blk")
    run_place = index % min(4, lax.axis_size("blk"))
    beyond = index - (ranks - 2) * lax.axis_size("blk")
    far_turns = (run_place == 1) | (beyond == 0)
    near_turns = ((run_place == 0) & (rank % 2 == 1)) | (beyond == 0)
    place = jnp.stack([index * tokens, far_turns, near_turns]).astype(jnp.int32)
    start = lax.dynamic_slice_in_dim(doc_start, rank, 1, 0)
    bf16, f32 = jnp.bfloat16, jnp.float32

    wide, both = (tokens, kv_width), (2 * tokens, kv_width)
    near, far = call(pair_kernel, "pair", [(both, bf16), (wide, bf16)], keys, values, flops=0)
    near, near_fixed = passed_on(near, 1)
    far, far_fixed = passed_on(far, 2)
    sent = (ranks, tokens + PAD, attn_out.shape[2])
    (packed,) = call(
        pack_kernel, "pack", [(sent, bf16)], log_norm, in_hbm=(attn_out,), out_hbm=1, flops=0, limit=60,
        scratch=[pltpu.VMEM(sent, bf16), pltpu.SemaphoreType.DMA((2, ranks))])
    packed = lax.all_to_all(packed, "ulysses", split_axis=0, concat_axis=0, tiled=True)

    unit = 2 * heads * 8 * half * half * DH
    packed_scratch = [pltpu.VMEM(packed.shape, bf16), pltpu.SemaphoreType.DMA((2 + kv_width // DH,))]
    r_far, r_near, key_halo, ds_top, ds_low = call(
        halo_kernel, "halo_grads",
        [(wide, bf16), (both, bf16), ((3 * half, kv_width), bf16), ((3 * half, heads * half), bf16),
         ((tokens, heads * half), bf16)],
        place, start, queries, grad_out, in_hbm=(far, far_fixed, near, near_fixed, packed), flops=3 * unit,
        scratch=[pltpu.VMEM(wide, bf16), pltpu.VMEM(both, bf16)] + packed_scratch)
    r_far = shifted(r_far, -2)
    count, slow = ranks * lax.axis_size("blk"), (ranks - 2) * lax.axis_size("blk")
    back = [(b, b - 1 if b != slow else count - 1) for b in range(1, count)]
    r_near = lax.ppermute(r_near, AXES, back)
    dk_own, dv_own, grad_queries = call(
        own_kernel, "own_grads", [(wide, f32), (wide, f32), (queries.shape, bf16)],
        place, start, queries, grad_out, keys, values, key_halo, ds_top, ds_low, in_hbm=(packed,), flops=3 * unit,
        scratch=packed_scratch)
    r_near, r_far, dk_own = lax.optimization_barrier((r_near, r_far, dk_own))
    relayed = lax.ppermute(r_near, AXES, [(count - 1, slow - 1)])
    r_near = jnp.where(index == slow - 1, relayed, jnp.where(index == count - 1, jnp.zeros_like(r_near), r_near))
    r_far = r_far.astype(f32)

    def total(own, near_part, far_part):
        return (own + near_part.astype(f32) + jnp.pad(far_part, ((half, 0), (0, 0)))).astype(bf16)

    return (grad_queries, total(dk_own, r_near[:tokens], r_far[:half]), total(dv_own, r_near[tokens:], r_far[half:]))


def solution(mesh):
    tokens_spec = P(AXES, None)
    return jax.shard_map(
        body,
        mesh=mesh,
        in_specs=(tokens_spec,) * 4 + (P(None, "blk", "ulysses"), P(None, "ulysses", "blk"), P(None, "blk")),
        out_specs=(tokens_spec,) * 3,
        check_vma=False,
    )
```

```python
import jax
import jax.numpy as jnp
from jax import lax
from jax.experimental import pallas as pl
from jax.experimental.pallas import tpu as pltpu
from jax.sharding import PartitionSpec as P

DH = 128
AXES = ("ulysses", "blk")
LOG2E = 1.4426950408889634
SCALE = DH**-0.5
RUN = 4
PAD = 16


def shifted(value, steps):
    count = lax.axis_size("ulysses") * lax.axis_size("blk")
    pairs = [(s, s + steps) for s in range(count) if 0 <= s + steps < count]
    return lax.ppermute(value, AXES, pairs)


def routes(steps):
    ranks, blocks = lax.axis_size("ulysses"), lax.axis_size("blk")
    run = min(4, blocks)
    direct, across = [], []
    for source in range(ranks * blocks - steps):
        target = source + steps
        rank, place = divmod(source, blocks)
        if target == (ranks - 2) * blocks:
            direct.append((source, 0))
            across.append((0, target))
        elif place % run + steps == run + steps - 1 and (steps > 1 or target // blocks % 2 == 1):
            middle = (rank if steps > 1 else rank | 1) * blocks + place - run + steps
            direct.append((source, middle))
            across.append((middle, target))
        else:
            direct.append((source, target))
    return direct, across


def passed_on(value, steps):
    direct, across = routes(steps)
    arrived = lax.ppermute(value, AXES, direct)
    return arrived, lax.ppermute(arrived, AXES, across)


def dot(a, b, dims):
    return lax.dot_general(a, b, (dims, ((), ())), preferred_element_type=jnp.float32)


def pair_kernel(k_ref, v_ref, near_ref, far_ref):
    tokens = k_ref.shape[0]
    half = tokens // 2
    near_ref[:tokens] = k_ref[...]
    near_ref[tokens:] = v_ref[...]
    far_ref[:half] = k_ref[half:]
    far_ref[half:] = v_ref[half:]


def pack_kernel(log_ref, o_hbm, packed_hbm, packed, sems):
    count, per, tokens = log_ref.shape
    half = tokens // 2
    loads = [pltpu.make_async_copy(o_hbm.at[c], packed.at[c, pl.ds(0, tokens)], sems.at[0, c]) for c in range(count)]
    stores = [pltpu.make_async_copy(packed.at[c], packed_hbm.at[c], sems.at[1, c]) for c in range(count)]
    for load in loads:
        load.start()
    lane = lax.broadcasted_iota(jnp.int32, (1, tokens), 1)
    for c in range(count):
        rows = []
        for a in range(0, per, 2):
            one, two = log_ref[c, a : a + 1, :], log_ref[c, a + 1 : a + 2, :]
            rows.append(jnp.where(lane < half, one, pltpu.roll(two, half, 1)))
            rows.append(jnp.where(lane < half, pltpu.roll(one, half, 1), two))
        left = jnp.concatenate(rows, axis=1)
        terms = []
        for _ in range(3):
            term = left.astype(jnp.bfloat16).astype(jnp.float32)
            left = left - term
            terms.append(term)
        terms.append(jnp.zeros((PAD - 3, left.shape[1]), jnp.float32))
        packed[c, tokens:] = jnp.concatenate(terms, axis=0).astype(jnp.bfloat16)
        loads[c].wait()
        stores[c].start()
    for store in stores:
        store.wait()


def head_cols(ref, rows, head):
    return ref[rows, head * DH : (head + 1) * DH]


def stacked_heads(ref, rows, heads):
    return jnp.concatenate([head_cols(ref, rows, h) for h in heads], axis=0)


def out_rows(ref, rows, heads, per):
    return jnp.concatenate([ref[h // per, rows, h % per * DH : (h % per + 1) * DH] for h in heads], axis=0)


def mask_bias(place_ref, start_ref, first_key, first_query, span, half):
    tokens = 2 * half
    key = lax.broadcasted_iota(jnp.int32, (span, tokens), 0) + first_key
    lane = lax.broadcasted_iota(jnp.int32, (span, tokens), 1)
    query = lax.rem(lane, half) + first_query
    start = start_ref[...] - place_ref[0]
    low = lax.broadcasted_iota(jnp.int32, start.shape, 1) < half
    moved = pltpu.roll(start, half, 1)
    start = jnp.where(low, moved, start) if first_query else jnp.where(low, start, moved)
    allowed = (key <= query) & (key > query - 3 * tokens // 2) & (key >= start)
    return jnp.where(allowed, 0.0, -jnp.inf)


def weights_of(keys, q_rows, bias, rows):
    shift = jnp.concatenate([bias - row for row in rows], axis=1)
    return jnp.exp2(dot(keys, q_rows, ((1,), (1,))) * (SCALE * LOG2E) + shift)


def centre_cols(g_rows, o_rows):
    prod = g_rows.astype(jnp.float32) * o_rows.astype(jnp.float32)
    prod = prod + pltpu.roll(prod, DH // 2, 1)
    head = prod.astype(jnp.bfloat16).astype(jnp.float32)
    lane = lax.broadcasted_iota(jnp.int32, prod.shape, 1)
    return jnp.where(lane < DH // 2, head, prod - head).astype(jnp.bfloat16)


def score_grads(weights, vals, g_rows, o_rows):
    vals = jnp.concatenate([vals, jnp.full(vals.shape, -1.0, vals.dtype)], axis=1)
    both = jnp.concatenate([g_rows, centre_cols(g_rows, o_rows)], axis=1)
    return (weights * dot(vals, both, ((1,), (1,)))).astype(jnp.bfloat16)


def log_terms(packed_ref, ranks, tokens):
    logs = {}
    for r in ranks:
        terms = packed_ref[r, tokens : tokens + PAD, :].astype(jnp.float32)
        logs[r] = LOG2E * (terms[0:1] + terms[1:2] + terms[2:3])
    return logs


def run_grads(q_ref, g_ref, packed_ref, logs, side, heads, per, keys, vals, bias):
    half = q_ref.shape[0] // 2
    rows = slice(side * half, (side + 1) * half)
    shifts = []
    for h in heads[::2]:
        at = (h % per + side) * DH
        shifts.append(logs[h // per][:, at : at + DH])
    q_rows, g_rows = stacked_heads(q_ref, rows, heads), stacked_heads(g_ref, rows, heads)
    weights = weights_of(keys, q_rows, bias, shifts)
    dscore = score_grads(weights, vals, g_rows, out_rows(packed_ref, rows, heads, per))
    return weights.astype(jnp.bfloat16), dscore, q_rows, g_rows


def start_all(pairs, sems, first):
    copies = [pltpu.make_async_copy(a, b, sems.at[first + i]) for i, (a, b) in enumerate(pairs)]
    for copy in copies:
        copy.start()
    return copies


def packed_moves(packed_hbm, packed_ref, kv_heads):
    ranks = packed_ref.shape[0] // kv_heads
    return [(packed_hbm.at[pl.ds(kv * ranks, ranks)], packed_ref.at[pl.ds(kv * ranks, ranks)]) for kv in range(kv_heads)]


def halo_kernel(place_ref, start_ref, q_ref, g_ref, far_hbm, far_fixed, near_hbm, near_fixed, packed_hbm,
                far_out, near_out, keys_out, ds_top, ds_low, far_ref, near_ref, packed_ref, sems):
    tokens, width = q_ref.shape
    half = tokens // 2
    kv_heads = far_ref.shape[1] // DH
    group = width // DH // kv_heads
    per = width // DH // packed_ref.shape[0]
    sources = ((far_hbm, far_fixed, far_ref), (near_hbm, near_fixed, near_ref))
    for i, (direct, fixed, target) in enumerate(sources):
        staged = place_ref[1 + i] == 1
        pl.when(staged)(pltpu.make_async_copy(fixed, target, sems.at[i]).start)
        pl.when(jnp.logical_not(staged))(pltpu.make_async_copy(direct, target, sems.at[i]).start)
    copies = start_all(packed_moves(packed_hbm, packed_ref, kv_heads), sems, 2)
    biases = (mask_bias(place_ref, start_ref, -3 * half, 0, 3 * half, half),
              mask_bias(place_ref, start_ref, -2 * half, half, tokens, half))
    for i, (direct, _, target) in enumerate(sources):
        pltpu.make_async_copy(direct, target, sems.at[i]).wait()
    keys_out[:half] = far_ref[:half]
    keys_out[half:] = near_ref[:tokens]
    for kv in range(kv_heads):
        copies[kv].wait()
        logs = log_terms(packed_ref, range(kv * group // per, (kv + 1) * group // per), tokens)
        cols = slice(kv * DH, (kv + 1) * DH)
        k_near, v_near = near_ref[:tokens, cols], near_ref[tokens:, cols]
        keys = (jnp.concatenate([far_ref[:half, cols], k_near], axis=0), k_near)
        vals = (jnp.concatenate([far_ref[half:, cols], v_near], axis=0), v_near)
        sums = []
        for side, ds_ref in enumerate((ds_top, ds_low)):
            val_sum = key_sum = 0.0
            for first in range(kv * group, (kv + 1) * group, RUN):
                weights, dscore, q_rows, g_rows = run_grads(
                    q_ref, g_ref, packed_ref, logs, side, range(first, first + RUN), per, keys[side], vals[side], biases[side])
                val_sum += dot(weights, g_rows, ((1,), (0,)))
                key_sum += dot(dscore, q_rows, ((1,), (0,)))
                ds_ref[:, first * half : (first + RUN) * half] = dscore
            sums.append((key_sum * SCALE, val_sum))
        for i in range(2):
            one, two = sums[0][i], sums[1][i]
            far_out[i * half : (i + 1) * half, cols] = one[:half].astype(jnp.bfloat16)
            near_out[i * tokens : (i + 1) * tokens, cols] = (one[half:] + two).astype(jnp.bfloat16)


def own_kernel(place_ref, start_ref, q_ref, g_ref, k_own, v_own, halo_ref, ds_top, ds_low, packed_hbm,
               dk_own, dv_own, dq_ref, packed_ref, sems):
    tokens, width = q_ref.shape
    half = tokens // 2
    kv_heads = k_own.shape[1] // DH
    group = width // DH // kv_heads
    per = width // DH // packed_ref.shape[0]
    copies = start_all(packed_moves(packed_hbm, packed_ref, kv_heads), sems, 0)
    biases = (mask_bias(place_ref, start_ref, 0, 0, half, half), mask_bias(place_ref, start_ref, 0, half, tokens, half))
    for kv in range(kv_heads):
        copies[kv].wait()
        logs = log_terms(packed_ref, range(kv * group // per, (kv + 1) * group // per), tokens)
        cols = slice(kv * DH, (kv + 1) * DH)
        sums = []
        for side, ds_ref in enumerate((ds_top, ds_low)):
            keys, vals = k_own[: (side + 1) * half, cols], v_own[: (side + 1) * half, cols]
            all_keys = jnp.concatenate([halo_ref[side * half :, cols], keys], axis=0)
            val_sum = key_sum = 0.0
            for first in range(kv * group, (kv + 1) * group, RUN):
                weights, dscore, q_rows, g_rows = run_grads(
                    q_ref, g_ref, packed_ref, logs, side, range(first, first + RUN), per, keys, vals, biases[side])
                val_sum += dot(weights, g_rows, ((1,), (0,)))
                key_sum += dot(dscore, q_rows, ((1,), (0,)))
                dscore = jnp.concatenate([ds_ref[:, first * half : (first + RUN) * half], dscore], axis=0)
                grad_q = (dot(dscore, all_keys, ((0,), (0,))) * SCALE).astype(jnp.bfloat16)
                for i in range(RUN):
                    out = slice((first + i) * DH, (first + i + 1) * DH)
                    dq_ref[side * half : (side + 1) * half, out] = grad_q[i * half : (i + 1) * half]
            sums.append((key_sum * SCALE, val_sum))
        for i, own in enumerate((dk_own, dv_own)):
            one, two = sums[0][i], sums[1][i]
            own[:half, cols] = one + two[:half]
            own[half:, cols] = two[half:]


def call(kernel, name, outs, *args, flops, in_hbm=(), out_hbm=0, scratch=(), limit=24):
    smem = pl.BlockSpec(memory_space=pltpu.SMEM)
    vmem = pl.BlockSpec(memory_space=pltpu.VMEM)
    hbm = pl.BlockSpec(memory_space=pl.ANY)
    return pl.pallas_call(
        kernel,
        in_specs=[smem if a.ndim == 1 else vmem for a in args] + [hbm] * len(in_hbm),
        out_specs=[vmem] * (len(outs) - out_hbm) + [hbm] * out_hbm,
        out_shape=[jax.ShapeDtypeStruct(s, d) for s, d in outs],
        compiler_params=pltpu.CompilerParams(vmem_limit_bytes=limit * 1024 * 1024),
        cost_estimate=pl.CostEstimate(flops=flops, bytes_accessed=4 << 20, transcendentals=1 << 20),
        scratch_shapes=scratch,
        name=name,
    )(*args, *in_hbm)


def body(queries, keys, values, grad_out, attn_out, log_norm, doc_start):
    tokens, width = queries.shape
    kv_width = keys.shape[1]
    half = tokens // 2
    heads = width // DH
    ranks = lax.axis_size("ulysses")
    rank = lax.axis_index("ulysses")
    index = rank * lax.axis_size("blk") + lax.axis_index("blk")
    run_place = index % min(4, lax.axis_size("blk"))
    beyond = index - (ranks - 2) * lax.axis_size("blk")
    far_turns = (run_place == 1) | (beyond == 0)
    near_turns = ((run_place == 0) & (rank % 2 == 1)) | (beyond == 0)
    place = jnp.stack([index * tokens, far_turns, near_turns]).astype(jnp.int32)
    start = lax.dynamic_slice_in_dim(doc_start, rank, 1, 0)
    bf16, f32 = jnp.bfloat16, jnp.float32

    wide, both = (tokens, kv_width), (2 * tokens, kv_width)
    near, far = call(pair_kernel, "pair", [(both, bf16), (wide, bf16)], keys, values, flops=0)
    near, near_fixed = passed_on(near, 1)
    far, far_fixed = passed_on(far, 2)
    sent = (ranks, tokens + PAD, attn_out.shape[2])
    (packed,) = call(
        pack_kernel, "pack", [(sent, bf16)], log_norm, in_hbm=(attn_out,), out_hbm=1, flops=0, limit=60,
        scratch=[pltpu.VMEM(sent, bf16), pltpu.SemaphoreType.DMA((2, ranks))])
    packed = lax.all_to_all(packed, "ulysses", split_axis=0, concat_axis=0, tiled=True)

    unit = 2 * heads * 8 * half * half * DH
    packed_scratch = [pltpu.VMEM(packed.shape, bf16), pltpu.SemaphoreType.DMA((2 + kv_width // DH,))]
    r_far, r_near, key_halo, ds_top, ds_low = call(
        halo_kernel, "halo_grads",
        [(wide, bf16), (both, bf16), ((3 * half, kv_width), bf16), ((3 * half, heads * half), bf16),
         ((tokens, heads * half), bf16)],
        place, start, queries, grad_out, in_hbm=(far, far_fixed, near, near_fixed, packed), flops=3 * unit,
        scratch=[pltpu.VMEM(wide, bf16), pltpu.VMEM(both, bf16)] + packed_scratch)
    r_far = shifted(r_far, -2)
    count, slow = ranks * lax.axis_size("blk"), (ranks - 2) * lax.axis_size("blk")
    back = [(b, b - 1 if b != slow else count - 1) for b in range(1, count)]
    r_near = lax.ppermute(r_near, AXES, back)
    dk_own, dv_own, grad_queries = call(
        own_kernel, "own_grads", [(wide, f32), (wide, f32), (queries.shape, bf16)],
        place, start, queries, grad_out, keys, values, key_halo, ds_top, ds_low, in_hbm=(packed,), flops=3 * unit,
        scratch=packed_scratch)
    r_near, r_far, dk_own = lax.optimization_barrier((r_near, r_far, dk_own))
    relayed = lax.ppermute(r_near, AXES, [(count - 1, slow - 1)])
    direct, through = (index != slow - 1) & (index != count - 1), index == slow - 1
    r_far = r_far.astype(f32)

    def total(own, part, far_part):
        near_part = jnp.where(direct, r_near[part].astype(f32), 0.0)
        near_part = jnp.where(through, relayed[part].astype(f32), near_part)
        return (own + near_part + jnp.pad(far_part, ((half, 0), (0, 0)))).astype(bf16)

    return (grad_queries, total(dk_own, slice(0, tokens), r_far[:half]), total(dv_own, slice(tokens, 2 * tokens), r_far[half:]))


def solution(mesh):
    tokens_spec = P(AXES, None)
    return jax.shard_map(
        body,
        mesh=mesh,
        in_specs=(tokens_spec,) * 4 + (P(None, "blk", "ulysses"), P(None, "ulysses", "blk"), P(None, "blk")),
        out_specs=(tokens_spec,) * 3,
        check_vma=False,
    )
```
